32 devices in a mesh: variant: 2 (over x), elem: 4 (over y, core), sub: 4 (over z).
Axes of the slice: x: 2, y: 2, z: 4, core: 2. Of those that a mesh axis runs over, the one named last changes fastest.
Arguments:
- right_side: float32 [8192, 512], P(('variant', 'elem', 'sub')), parts along dimension 0, may hold values from -16 to 16, as said below
- smoother_scale: float32 [8192, 512], P(('variant', 'elem', 'sub')), parts along dimension 0, may hold values from 0.5 to 1.5
- helmholtz: float32 [8192, 512], P(('variant', 'elem', 'sub')), parts along dimension 0, may hold values from 0.5 to 2
- geometry: float32 [3, 8192, 512], P(None, ('variant', 'elem', 'sub')), parts along dimension 1, may hold values from 0.001 to 0.01
- coarse_inverse: float32 [8, 1024, 1024], P(('variant', 'elem'), 'sub'), parts along dimension 0, may hold values from -1.25 to 6.25, as said below
- vertex_ids: int32 [8, 4096], P(None, ('elem', 'sub')), may hold values from 0 to 1023
- face_slot: int32 [16, 4, 192], P(('elem', 'sub')), may hold values from 0 to 1535, as said below
- face_partner: int32 [16, 4, 192], P(('elem', 'sub')), may hold values from 0 to 191, as said below
Outputs:
- solution: float32 [8192, 512], P(('variant', 'elem', 'sub')), parts along dimension 0
- residual: float32 [8192, 512], P(('variant', 'elem', 'sub')), parts along dimension 0
- direction: float32 [8192, 512], P(('variant', 'elem', 'sub')), parts along dimension 0
The draws below stay inside these ranges and needn't reach their ends.
There are 2 independent parts, one for each index of `variant`. The reference program is written for one: setup_inputs(seed, part) draws one part's arguments, and reference() takes and returns one part's arrays. A program takes and returns all parts, laid end to end along the dimension named above; an argument that names none is the same for every part. Nothing has to cross between parts.
Inputs may be any that keep to these rules, and one draw needn't show every extreme that they name: `right_side`: Right-hand side values; their size differs from device to device. `coarse_inverse`: each matrix is symmetric. `vertex_ids`: vertex v of a coarse group belongs to index v // 256 of sub. Each device's corners may name any vertex of its group. `face_slot`: the 768 entries of one device are all different. For every device and section the row is a permutation of 0 to 191, and the pairing is mutual: face_partner[d XOR 2^b, b, face_partner[d, b, k]] = k.
All inputs are finite; a program needn't handle non-finite values.
Results may differ from the reference program's by a relative error of at most 0.0003.
Values sent between devices are 32-bit elements; how exact they have to be, the bound alone decides.
A program may use at most 128 MiB of HBM per device.

```python
import math
import jax
import jax.numpy as jnp
import numpy as np
from jax import lax

NP = 8
ITERS = 2
E_DEV = 256
FB = 192
PDEV = 16
SECTIONS = 4
ELEMS = 4096
NV = 1024
N_ELEM = 4


def draw_right_side(key, part):
    key = jax.random.fold_in(key, 3)
    device_of = jnp.arange(ELEMS, dtype=jnp.int32) // E_DEV
    rise = device_of.astype(jnp.float32) / max(PDEV - 1, 1)
    values = jnp.clip(jax.random.normal(key, (ELEMS, NP * NP * NP), jnp.float32), -5.0, 5.0)
    return values * (3.0 ** rise)[:, None]


def draw_coarse_inverse(key, part):
    key = jax.random.fold_in(key, 5)
    jitter = jax.random.uniform(jax.random.fold_in(key, 1), (N_ELEM, NV, NV), jnp.float32, -1.0, 1.0)
    diag_values = jax.random.uniform(jax.random.fold_in(key, 2), (N_ELEM, NV), jnp.float32, 4.0, 6.0)
    couple = jax.random.uniform(jax.random.fold_in(key, 3), (N_ELEM, NV), jnp.float32, 0.25, 1.0)
    row_index = jnp.arange(NV, dtype=jnp.int32)[:, None]
    col_index = jnp.arange(NV, dtype=jnp.int32)[None, :]
    upper_band = jnp.where((col_index == row_index + 1)[None, :, :], -couple[:, :, None], 0.0)
    coupling = upper_band + jnp.swapaxes(upper_band, 1, 2)
    diagonal_part = jnp.where((col_index == row_index)[None, :, :], diag_values[:, :, None], 0.0)
    scale_factor = 0.5 / NV ** 0.5
    return (jitter + jnp.swapaxes(jitter, 1, 2)) * scale_factor + coupling + diagonal_part


def draw_face_slot(key, part):
    key = jax.random.fold_in(key, 7)
    sides_total = 6 * E_DEV
    listed = SECTIONS * FB

    def one_device(device):
        inner = jax.random.permutation(jax.random.fold_in(key, device), sides_total - 2) + 1
        chosen = jnp.concatenate([jnp.array([0, sides_total - 1], jnp.int32), inner[:listed - 2].astype(jnp.int32)])
        mixed = jax.random.permutation(jax.random.fold_in(key, device + PDEV), chosen)
        return mixed.reshape(SECTIONS, FB)
    return jax.vmap(one_device)(jnp.arange(PDEV, dtype=jnp.int32))


def draw_face_partner(key, part):
    key = jax.random.fold_in(key, 9)

    def one_pair(device, section):
        upper = jnp.bitwise_and(jnp.right_shift(device, section), 1)
        lower = device - jnp.left_shift(upper, section)
        order = jax.random.permutation(jax.random.fold_in(jax.random.fold_in(key, lower), section), FB).astype(jnp.int32)
        return jnp.where(upper == 1, jnp.argsort(order).astype(jnp.int32), order)
    devices = jnp.arange(PDEV, dtype=jnp.int32)
    sections = jnp.arange(SECTIONS, dtype=jnp.int32)
    return jax.vmap(lambda device: jax.vmap(lambda section: one_pair(device, section))(sections))(devices)


def with_ends(values, stream_key, smallest, high):
    shape = values.shape
    spot = [jax.random.randint(jax.random.fold_in(stream_key, axis), (), 0, shape[axis]) for axis in range(len(shape))]
    values = values.at[tuple(spot)].set(smallest)
    longest = shape.index(max(shape))
    spot[longest] = (spot[longest] + 1) % shape[longest]
    return values.at[tuple(spot)].set(high)


def block_scale(rng, shape, shards, least, top_value):
    factor_of = 1.0
    for position, shards_of in shards:
        draws = jax.random.uniform(jax.random.fold_in(jax.random.fold_in(rng, 6), position), (shards_of,), jnp.float32, least / len(shards), top_value / len(shards))
        factor_of = factor_of * jnp.repeat(jnp.exp(draws), shape[position] // shards_of).reshape((-1,) + (1,) * (len(shape) - 1 - position))
    return factor_of


def setup_inputs(seed: int = 0, part: int = 0) -> dict:
    streams_of = jax.random.split(jax.random.key(seed), 9)
    own_keys = jax.random.split(jax.random.fold_in(streams_of[8], part), 9)
    return {
        "right_side": draw_right_side(jax.random.fold_in(jax.random.fold_in(streams_of[8], part), 71), part),
        "smoother_scale": jnp.clip(jnp.exp(math.log(1.5) - 1.0986123 * jax.random.uniform(own_keys[1], (ELEMS, NP * NP * NP), jnp.float32) ** block_scale(own_keys[1], (ELEMS, NP * NP * NP), ((0, 16),), -0.2, 0.2)), 0.5, 1.5),
        "helmholtz": jnp.clip(jnp.exp(math.log(2.0) - 1.3862944 * jax.random.uniform(own_keys[2], (ELEMS, NP * NP * NP), jnp.float32) ** block_scale(own_keys[2], (ELEMS, NP * NP * NP), ((0, 16),), -0.2, 0.2)), 0.5, 2.0),
        "geometry": jnp.clip(jnp.exp(math.log(0.01) - 2.30258502 * jax.random.uniform(own_keys[3], (3, ELEMS, NP * NP * NP), jnp.float32) ** block_scale(own_keys[3], (3, ELEMS, NP * NP * NP), ((1, 16),), -0.2, 0.2)), 0.001, 0.01),
        "coarse_inverse": draw_coarse_inverse(jax.random.fold_in(jax.random.fold_in(streams_of[8], part), 71), part),
        "vertex_ids": with_ends(jax.random.randint(streams_of[5], (8, ELEMS), 0, NV), jax.random.fold_in(streams_of[5], 1), 0, NV - 1).astype(jnp.int32),
        "face_slot": draw_face_slot(jax.random.fold_in(streams_of[8], 71), part),
        "face_partner": draw_face_partner(jax.random.fold_in(streams_of[8], 71), part),
    }


PENALTY = 1.0
SMOOTH = 0.125


def derivative_table(points):
    nodes = -np.cos(np.pi * np.arange(points) / (points - 1))
    end_weights = np.ones(points)
    end_weights[0] = 2.0
    end_weights[-1] = 2.0
    table = np.zeros((points, points))
    for row_index in range(points):
        for column in range(points):
            if row_index != column:
                table[row_index, column] = end_weights[row_index] / end_weights[column] * (-1.0) ** (row_index + column) / (nodes[row_index] - nodes[column])
        table[row_index, row_index] = -np.sum(table[row_index])
    return nodes, table


def spectral_tables(points):
    nodes, deriv = derivative_table(points)
    unit = np.eye(points)
    slow_op = np.kron(deriv, np.kron(unit, unit))
    middle_op = np.kron(unit, np.kron(deriv, unit))
    fast_op = np.kron(unit, np.kron(unit, deriv))
    operators = np.stack([slow_op, middle_op, fast_op])
    hats = np.stack([(1.0 - nodes) / 2.0, (1.0 + nodes) / 2.0])
    turned = hats.T
    raw_hats = turned[:, None, None, :, None, None] * turned[None, :, None, None, :, None] * turned[None, None, :, None, None, :]
    raw_hats = raw_hats.reshape(points ** 3, 8)
    corner = raw_hats / raw_hats.sum(axis=0, keepdims=True)
    grid = np.arange(points ** 3).reshape(points, points, points)
    sides = np.stack([grid[0].ravel(), grid[-1].ravel(), grid[:, 0].ravel(), grid[:, -1].ravel(), grid[:, :, 0].ravel(), grid[:, :, -1].ravel()])
    return jnp.asarray(operators, jnp.float32), jnp.asarray(corner, jnp.float32), jnp.asarray(raw_hats, jnp.float32), sides


def stiffness(field, geometry, helmholtz, operators):
    total = helmholtz * field
    for direction_index in range(3):
        slope = jnp.dot(field, operators[direction_index].T, precision=lax.Precision.HIGHEST)
        total = total + jnp.dot(geometry[direction_index] * slope, operators[direction_index], precision=lax.Precision.HIGHEST)
    return total


def face_values(field, slots, sides):
    stacked = jnp.concatenate([field[:, sides[side_number]] for side_number in range(6)], axis=0)
    return jnp.take(stacked, slots, axis=0)


def spread_faces(values, slots, sides, count):
    square = sides.shape[1]
    flat = jnp.zeros((6 * count, square), values.dtype).at[slots.reshape(-1)].add(values.reshape(-1, square))
    result = jnp.zeros((count, square * NP), values.dtype)
    for side_number in range(6):
        result = result.at[:, sides[side_number]].add(flat[side_number * count:(side_number + 1) * count])
    return result


def neighbour_sum(field, face_slot, face_partner, sides):
    devices, sections, width = face_slot.shape
    blocks = field.reshape(devices, -1, field.shape[-1])
    count = blocks.shape[1]
    faces = jax.vmap(lambda block, slots: face_values(block, slots, sides))(blocks, face_slot)
    own_index = jnp.arange(devices, dtype=jnp.int32)[:, None]
    section_index = jnp.arange(sections, dtype=jnp.int32)[None, :]
    partner_device = jnp.bitwise_xor(own_index, jnp.left_shift(jnp.int32(1), section_index))
    received = faces[partner_device, section_index]
    aligned = jnp.take_along_axis(received, face_partner[:, :, :, None], axis=2)
    spread = jax.vmap(lambda values, slots: spread_faces(values, slots, sides, count))(aligned, face_slot)
    return spread.reshape(field.shape)


def coarse_term(resid, vertex_ids, coarse_inverse, corner, prolong):
    corners = jnp.dot(resid, corner, precision=lax.Precision.HIGHEST)
    groups = coarse_inverse.shape[0]
    count = coarse_inverse.shape[1]
    group_of = jnp.arange(resid.shape[0], dtype=jnp.int32) // (resid.shape[0] // groups)
    flat_ids = vertex_ids + group_of[None, :] * count
    coarse_rhs = jax.ops.segment_sum(corners.T.reshape(-1), flat_ids.reshape(-1), num_segments=groups * count).reshape(groups, count)
    solved = jnp.einsum('gij,gj->gi', coarse_inverse, coarse_rhs, precision=lax.Precision.HIGHEST)
    picked = jnp.take(solved.reshape(-1), flat_ids, axis=0)
    return jnp.dot(picked.T, prolong.T, precision=lax.Precision.HIGHEST)


def reference(right_side, smoother_scale, helmholtz, geometry, coarse_inverse, vertex_ids, face_slot, face_partner):
    operators, corner, prolong, sides = spectral_tables(NP)
    devices, sections, width = face_slot.shape
    count = right_side.shape[0] // devices
    ones_faces = jnp.ones((devices, sections, width, sides.shape[1]), right_side.dtype)
    degree = jax.vmap(lambda values, slots: spread_faces(values, slots, sides, count))(ones_faces, face_slot).reshape(right_side.shape)

    def apply_operator(field):
        coupled = degree * field - neighbour_sum(field, face_slot, face_partner, sides)
        return stiffness(field, geometry, helmholtz, operators) + PENALTY * coupled

    def precondition(resid):
        scaled = smoother_scale * resid
        smooth = scaled - SMOOTH * (degree * scaled - neighbour_sum(scaled, face_slot, face_partner, sides))
        return smoother_scale * smooth + coarse_term(resid, vertex_ids, coarse_inverse, corner, prolong)

    solution = jnp.zeros_like(right_side)
    residual = right_side
    precond = precondition(residual)
    direction = precond
    rz_now = jnp.sum(residual * precond)
    for sweep in range(ITERS):
        image = apply_operator(direction)
        alpha = rz_now / jnp.sum(direction * image)
        solution = solution + alpha * direction
        residual = residual - alpha * image
        precond = precondition(residual)
        rz_next = jnp.sum(residual * precond)
        direction = precond + (rz_next / rz_now) * direction
        rz_now = rz_next
    return solution, residual, direction
```

```python
import functools

import jax
import jax.numpy as jnp
import ml_dtypes
import numpy as np
from jax import lax
from jax.experimental import pallas as pl
from jax.experimental.pallas import tpu as pltpu
from jax.sharding import PartitionSpec as P

NP = 8
PTS = NP**3
SQ = NP * NP
SMOOTH = 0.125
MESH = pl.DeviceIdType.MESH
F32 = jnp.float32
BF16 = jnp.bfloat16


def derivative_table(points):
    nodes = -np.cos(np.pi * np.arange(points) / (points - 1))
    end_weights = np.ones(points)
    end_weights[0] = 2.0
    end_weights[-1] = 2.0
    table = np.zeros((points, points))
    for i in range(points):
        for j in range(points):
            if i != j:
                table[i, j] = (
                    end_weights[i] / end_weights[j] * (-1.0) ** (i + j) / (nodes[i] - nodes[j])
                )
        table[i, i] = -np.sum(table[i])
    return nodes, table


def halves(x):
    x = np.asarray(x, np.float32)
    hi = x.astype(ml_dtypes.bfloat16)
    lo = (x - hi.astype(np.float32)).astype(ml_dtypes.bfloat16)
    return hi, lo


def tables(nh):
    nodes, deriv = derivative_table(NP)
    unit = np.eye(NP)
    k0 = np.kron(deriv, np.eye(SQ))
    k1 = np.kron(np.eye(4), np.kron(deriv, unit))
    k2 = np.kron(np.eye(4 * NP), deriv)
    hats = np.stack([(1.0 - nodes) / 2.0, (1.0 + nodes) / 2.0]).T
    raw = (
        hats[:, None, None, :, None, None]
        * hats[None, :, None, None, :, None]
        * hats[None, None, :, None, None, :]
    ).reshape(PTS, 8)
    corner = raw / raw.sum(axis=0, keepdims=True)
    grid = np.arange(PTS).reshape(NP, NP, NP)
    inner = [grid[:, 0], grid[:, -1], grid[:, :, 0], grid[:, :, -1]]
    sel = np.zeros((PTS, 4 * SQ), np.float32)
    spread = np.zeros((4 * 2 * SQ, PTS), np.float32)
    for s, side in enumerate(inner):
        for j, p in enumerate(side.ravel()):
            sel[p, s * SQ + j] = 1.0
            spread[s * 2 * SQ + j, p] = 1.0
            spread[s * 2 * SQ + SQ + j, p] = 1.0
    k0h, k0l = halves(k0)
    k1h, k1l = halves(k1)
    k2h, k2l = halves(k2)
    wh, wl = halves(np.repeat(corner, nh, axis=1))
    w = np.concatenate([wh, wl], axis=1)
    hh, hl = halves(np.repeat(raw.T, nh, axis=0))
    hh = np.concatenate([hh, hh], axis=0)
    hl = np.concatenate([hl, hl], axis=0)
    one = ml_dtypes.bfloat16
    return (
        np.stack([k0h, k0l]),
        np.stack([k1h, k1l]),
        np.stack([k2h, k2l]),
        sel.astype(one),
        spread.astype(one),
        w,
        np.stack([hh, hl]),
    )


NN = (((1,), (0,)), ((), ()))
NT = (((1,), (1,)), ((), ()))
TN = (((0,), (0,)), ((), ()))


def mm(a, b, dims=NN):
    return lax.dot_general(a, b, dims, preferred_element_type=F32)


def split(x):
    hi = x.astype(BF16)
    lo = (x - hi.astype(F32)).astype(BF16)
    return hi, lo


def iota(shape, dim):
    return lax.broadcasted_iota(jnp.int32, shape, dim)


def kernel(
    n_elem, n_sub, sections, width, nh,
    rhs_ref, scale_ref, helm_ref, geo_ref, inv_ref, vid_ref, slot_ref, partner_ref, slots_ref,
    k0_ref, k1_ref, k2_ref, sel_ref, spread_ref, w_ref, hat_ref,
    x_ref, r_ref, d_ref,
    gather, scatter, stacked, arrived, degree, corner_low, corner_high, inv_half,
    fsend, frecv, part, solved_slots, total_slots,
    fsend_sem, frecv_sem, psend_sem, precv_sem, ssend_sem, srecv_sem, tsend_sem, trecv_sem,
):
    count = rhs_ref.shape[0]
    half = width // 2
    devices = n_elem * n_sub
    ch = 8 * nh
    elem = lax.axis_index("elem")
    sub = lax.axis_index("sub")
    me = elem * n_sub + sub

    def other(j):
        p = lax.rem(me + j, devices)
        return {"elem": lax.div(p, n_sub), "sub": lax.rem(p, n_sub)}

    barrier = pltpu.get_barrier_semaphore()

    def greet(j, carry):
        pl.semaphore_signal(barrier, inc=1, device_id=other(j), device_id_type=MESH)
        return carry

    lax.fori_loop(1, devices, greet, 0)

    low = iota((1, 128), 1) < SQ

    for b in range(sections):
        hit = partner_ref[b : b + 1, :] == iota((width, width), 0)
        order = jnp.sum(
            jnp.where(hit, slots_ref[b : b + 1, :].astype(F32), 0.0), axis=1, keepdims=True
        ).astype(jnp.int32)
        gather[b * width : (b + 1) * width, :] = jnp.where(
            order == iota((width, 6 * count), 1), 1.0, 0.0
        ).astype(BF16)
    for s in range(6):
        scatter[s * count : (s + 1) * count, :] = jnp.where(
            slot_ref[...] - s * count == iota((count, sections * width), 0), 1.0, 0.0
        ).astype(BF16)

    vid = vid_ref[...]
    vid_high = lax.div(vid, 128)
    vid_low = vid - 128 * vid_high
    wide = iota((8, 8 * 128), 1)
    expand_low = jnp.where(lax.div(wide, 128) == iota((8, 8 * 128), 0), 1.0, 0.0)
    spread_low = mm(vid_low.astype(F32), expand_low, TN).astype(jnp.int32)
    corner_low[...] = jnp.where(
        spread_low == lax.rem(iota((count, 8 * 128), 1), 128), 1.0, 0.0
    ).astype(BF16)
    pair = iota((8, 2 * ch), 1)
    expand_high = jnp.where(lax.div(lax.rem(pair, ch), nh) == iota((8, 2 * ch), 0), 1.0, 0.0)
    spread_high = mm(vid_high.astype(F32), expand_high, TN).astype(jnp.int32)
    corner_high[...] = jnp.where(spread_high == lax.rem(iota((count, 2 * ch), 1), nh), 1.0, 0.0)

    inv_h, inv_l = split(inv_ref[...])
    inv_half[0] = inv_h
    inv_half[1] = inv_l

    def scatter_faces():
        flat = mm(scatter[...], arrived[...])
        sides = [flat[s * count : (s + 1) * count, :] for s in range(6)]
        inner = jnp.concatenate(sides[2:], axis=1).astype(BF16)
        result = mm(inner, spread_ref[...])
        first = sides[0] + pltpu.roll(sides[0], SQ, 1)
        last = sides[1] + pltpu.roll(sides[1], SQ, 1)
        return jnp.concatenate(
            [
                result[:, :128] + jnp.where(low, first, 0.0),
                result[:, 128 : PTS - 128],
                result[:, PTS - 128 :] + jnp.where(low, 0.0, last),
            ],
            axis=1,
        )

    arrived[...] = jnp.broadcast_to(jnp.where(low, 1.0, 0.0), arrived.shape).astype(BF16)
    degree[...] = scatter_faces()

    pl.semaphore_wait(barrier, devices - 1)

    pending = []

    def send_faces(step, v):
        hi = v.astype(BF16)
        hi_f = hi.astype(F32)
        lo_f = v - hi_f
        picked = mm(jnp.concatenate([hi, lo_f.astype(BF16)], axis=0), sel_ref[...])

        def lower(h, l):
            return jnp.where(low, h, pltpu.roll(l, SQ, 1)).astype(BF16)

        def upper(h, l):
            return jnp.where(low, pltpu.roll(h, SQ, 1), l).astype(BF16)

        stacked[0:count, :] = lower(hi_f[:, :128], lo_f[:, :128])
        stacked[count : 2 * count, :] = upper(hi_f[:, PTS - 128 :], lo_f[:, PTS - 128 :])
        for s in range(2):
            h = picked[:count, 128 * s : 128 * s + 128]
            l = picked[count:, 128 * s : 128 * s + 128]
            stacked[(2 + 2 * s) * count : (3 + 2 * s) * count, :] = lower(h, l)
            stacked[(3 + 2 * s) * count : (4 + 2 * s) * count, :] = upper(h, l)
        for b in reversed(range(sections)):
            rows = mm(gather[b * width : (b + 1) * width, :], stacked[...])
            rows = rows + pltpu.roll(rows, SQ, 1)
            fsend[step, b] = jnp.where(low, rows[:half], rows[half:])
            bit = lax.rem(lax.div(me, 2**b), 2)
            p = me + (1 - 2 * bit) * 2**b
            copy = pltpu.make_async_remote_copy(
                src_ref=fsend.at[step, b],
                dst_ref=frecv.at[step, b],
                send_sem=fsend_sem.at[step, b],
                recv_sem=frecv_sem.at[step, b],
                device_id={"elem": lax.div(p, n_sub), "sub": lax.rem(p, n_sub)},
                device_id_type=MESH,
            )
            copy.start()
            pending.append(copy)

    def neighbours(step):
        for b in reversed(range(sections)):
            pltpu.make_async_copy(
                frecv.at[step, b], frecv.at[step, b], frecv_sem.at[step, b]
            ).wait()
            v = frecv[step, b]
            hi = v.astype(BF16).astype(F32)
            lo = v - hi
            arrived[b * width : b * width + half, :] = jnp.where(
                low, hi, pltpu.roll(lo, SQ, 1)
            ).astype(BF16)
            arrived[b * width + half : (b + 1) * width, :] = jnp.where(
                low, pltpu.roll(hi, SQ, 1), lo
            ).astype(BF16)
        return scatter_faces()

    def to_sub_peers(step, slots, index_of, send_sem, recv_sem):
        for j in range(1, n_sub):
            copy = pltpu.make_async_remote_copy(
                src_ref=slots.at[step, index_of(0)],
                dst_ref=slots.at[step, index_of(j)],
                send_sem=send_sem.at[step, j],
                recv_sem=recv_sem.at[step, j],
                device_id={"elem": elem, "sub": lax.rem(sub + j, n_sub)},
                device_id_type=MESH,
            )
            copy.start()
            pending.append(copy)

    def wait_sub_peers(step, slots, recv_sem):
        for j in range(1, n_sub):
            pltpu.make_async_copy(slots.at[step, 0], slots.at[step, 0], recv_sem.at[step, j]).wait()

    def send_corners(step, r):
        hi, lo = split(r)
        y = mm(hi, w_ref[...]) + mm(lo, w_ref[...])
        y = (y + pltpu.roll(y, ch, 1)) * corner_high[...]
        hi = y.astype(BF16).astype(F32)
        both = jnp.where(iota((1, 2 * ch), 1) < ch, hi, y - hi).astype(BF16)
        products = mm(both, corner_low[...], TN)
        total = None
        for k in range(2):
            for c in range(8):
                piece = products[k * ch + c * nh : k * ch + (c + 1) * nh, 128 * c : 128 * c + 128]
                total = piece if total is None else total + piece
        part[step, 0] = total
        to_sub_peers(step, part, lambda j: j, psend_sem, precv_sem)

    def solve(step):
        wait_sub_peers(step, part, precv_sem)
        total = part[step, 0]
        for j in range(1, n_sub):
            total = total + part[step, j]
        hi = total.astype(BF16).astype(F32)
        lo = total - hi
        row_h = jnp.concatenate([hi[h : h + 1, :] for h in range(nh)], axis=1)
        row_l = jnp.concatenate([lo[h : h + 1, :] for h in range(nh)], axis=1)
        rows = jnp.concatenate([row_h, row_l, jnp.zeros((14, nh * 128), F32)], axis=0).astype(BF16)
        out = mm(rows, inv_half[0], NT) + mm(rows, inv_half[1], NT)
        out = out[0:1] + out[1:2]
        own = [out[:, 128 * k : 128 * k + 128] for k in range(out.shape[1] // 128)]
        own.append(jnp.zeros((8 - len(own), 128), F32))
        solved_slots[step, sub] = jnp.concatenate(own, axis=0)
        to_sub_peers(step, solved_slots, lambda j: sub, ssend_sem, srecv_sem)

    def coarse(step):
        wait_sub_peers(step, solved_slots, srecv_sem)
        each = nh // n_sub
        solved = jnp.concatenate([solved_slots[step, j, 0:each, :] for j in range(n_sub)], axis=0)
        hi = solved.astype(BF16).astype(F32)
        lo = solved - hi
        keep = lax.div(iota((ch, 8 * 128), 0), nh) == lax.div(iota((ch, 8 * 128), 1), 128)

        def blocks(x):
            column = jnp.concatenate([x] * 8, axis=0)
            return jnp.where(keep, jnp.concatenate([column] * 8, axis=1), 0.0).astype(BF16)

        spread = jnp.concatenate([blocks(hi), blocks(lo)], axis=0)
        picked = (mm(corner_low[...], spread, NT) * corner_high[...]).astype(BF16)
        return mm(picked, hat_ref[0]) + mm(picked, hat_ref[1])

    def local(v):
        n2 = PTS // 2
        hi, lo = split(v)
        k0h, k0l = k0_ref[0], k0_ref[1]

        def two(x):
            return jnp.concatenate([x[:, :n2], x[:, n2:]], axis=0)

        def three(h, l, kh, kl, dims):
            return mm(h, kh, dims) + mm(l, kh, dims) + mm(h, kl, dims)

        slope = geo_ref[0] * three(hi, lo, k0h, k0l, NT)
        sh, sl = split(slope)
        total = helm_ref[...] * v + three(sh, sl, k0h, k0l, NN)
        hi2, lo2 = two(hi), two(lo)
        rest = None
        for d, k in ((1, k1_ref), (2, k2_ref)):
            slope = two(geo_ref[d]) * three(hi2, lo2, k[0], k[1], NT)
            sh, sl = split(slope)
            piece = three(sh, sl, k[0], k[1], NN)
            rest = piece if rest is None else rest + piece
        return total + jnp.concatenate([rest[:count], rest[count:]], axis=1)

    def inner(a, b):
        return jnp.sum(a * b, axis=0, keepdims=True)

    def narrow(x):
        total = x[:, :128]
        for k in range(1, PTS // 128):
            total = total + x[:, 128 * k : 128 * k + 128]
        return total

    def send_totals(step, pairs):
        rows = [narrow(inner(a, b)) for a, b in pairs]
        rows.append(jnp.zeros((8 - len(rows), 128), F32))
        total_slots[step, 0] = jnp.concatenate(rows, axis=0)

        def start(j, carry):
            pltpu.make_async_remote_copy(
                src_ref=total_slots.at[step, 0],
                dst_ref=total_slots.at[step, j],
                send_sem=tsend_sem.at[step],
                recv_sem=trecv_sem.at[step],
                device_id=other(j),
                device_id_type=MESH,
            ).start()
            return carry

        lax.fori_loop(1, devices, start, 0)

    def totals(step, many):
        others = total_slots.at[step, pl.ds(1, devices - 1)]
        pltpu.make_async_copy(others, others, trecv_sem.at[step]).wait()
        whole = jnp.sum(total_slots[step], axis=0)
        sums = jnp.sum(whole, axis=1, keepdims=True)
        return [sums[k : k + 1] for k in range(many)]

    scale = scale_ref[...]

    def smooth_of(y, step):
        return scale * (y - SMOOTH * (degree[...] * y - neighbours(step)))

    def precondition(v, faces, step):
        y = scale * v
        send_corners(step, v)
        send_faces(faces, y)
        solve(step)
        smooth = smooth_of(y, faces)
        return smooth + coarse(step)

    def operator(v, step):
        send_faces(step, v)
        inside = local(v) + degree[...] * v
        return inside - neighbours(step)

    r0 = rhs_ref[...]
    z0 = precondition(r0, 0, 0)
    w0 = operator(z0, 1)
    send_totals(0, [(r0, z0), (z0, w0)])
    q0 = precondition(w0, 2, 1)
    rz0, dw0 = totals(0, 2)
    alpha0 = rz0 / dw0
    r1 = r0 - alpha0 * w0
    z1 = z0 - alpha0 * q0
    u1 = operator(z1, 3)
    send_totals(1, [(r1, z1), (z1, u1), (z1, w0), (z0, u1)])
    q1 = precondition(u1, 4, 2)
    rz1, zu, zw, du = totals(1, 4)
    beta0 = rz1 / rz0
    dw1 = zu + beta0 * (zw + du) + beta0 * beta0 * dw0
    alpha1 = rz1 / dw1
    d1 = z1 + beta0 * z0
    r2 = r1 - alpha1 * (u1 + beta0 * w0)
    z2 = z1 - alpha1 * (q1 + beta0 * q0)
    send_totals(2, [(r2, z2)])
    x_ref[...] = alpha0 * z0 + alpha1 * d1
    r_ref[...] = r2
    (rz2,) = totals(2, 1)
    d_ref[...] = z2 + (rz2 / rz1) * d1

    for copy in pending:
        copy.wait_send()
    for step in range(3):
        others = total_slots.at[step, pl.ds(1, devices - 1)]
        pltpu.make_async_copy(others, others, tsend_sem.at[step]).wait()


def on_device(
    n_elem, n_sub,
    right_side, smoother_scale, helmholtz, geometry, coarse_inverse, vertex_ids, face_slot, face_partner,
):
    count = right_side.shape[0]
    _, sections, width = face_slot.shape
    half = width // 2
    nv = coarse_inverse.shape[2]
    nh = nv // 128
    devices = n_elem * n_sub
    constants = [jnp.asarray(t) for t in tables(nh)]
    vmem = pl.BlockSpec(memory_space=pltpu.VMEM)
    field = jax.ShapeDtypeStruct((count, PTS), F32)
    dma = pltpu.SemaphoreType.DMA
    operands = (
        right_side, smoother_scale, helmholtz, geometry, coarse_inverse[0], vertex_ids,
        face_slot.reshape(1, sections * width), face_partner[0], face_slot[0], *constants,
    )
    return pl.pallas_call(
        functools.partial(kernel, n_elem, n_sub, sections, width, nh),
        out_shape=(field, field, field),
        in_specs=[vmem] * len(operands),
        out_specs=(vmem, vmem, vmem),
        scratch_shapes=[
            pltpu.VMEM((sections * width, 6 * count), BF16),
            pltpu.VMEM((6 * count, sections * width), BF16),
            pltpu.VMEM((6 * count, 128), BF16),
            pltpu.VMEM((sections * width, 128), BF16),
            pltpu.VMEM((count, PTS), F32),
            pltpu.VMEM((count, 8 * 128), BF16),
            pltpu.VMEM((count, 16 * nh), F32),
            pltpu.VMEM((2,) + coarse_inverse.shape[1:], BF16),
            pltpu.VMEM((5, sections, half, 128), F32),
            pltpu.VMEM((5, sections, half, 128), F32),
            pltpu.VMEM((3, n_sub, nh, 128), F32),
            pltpu.VMEM((3, n_sub, 8, 128), F32),
            pltpu.VMEM((3, devices, 8, 128), F32),
            dma((5, sections)),
            dma((5, sections)),
            dma((3, n_sub)),
            dma((3, n_sub)),
            dma((3, n_sub)),
            dma((3, n_sub)),
            dma((3,)),
            dma((3,)),
        ],
        compiler_params=pltpu.CompilerParams(
            collective_id=0, has_side_effects=True, vmem_limit_bytes=56 * 2**20
        ),
        cost_estimate=pl.CostEstimate(flops=2 * 10**10, bytes_accessed=8 * 10**6, transcendentals=0),
    )(*operands)


def solution(mesh):
    rows = P(("variant", "elem", "sub"), None)
    in_specs = (
        rows,
        rows,
        rows,
        P(None, ("variant", "elem", "sub"), None),
        P(("variant", "elem"), "sub", None),
        P(None, ("elem", "sub")),
        P(("elem", "sub"), None, None),
        P(("elem", "sub"), None, None),
    )
    body = functools.partial(on_device, mesh.shape["elem"], mesh.shape["sub"])
    return jax.shard_map(
        body, mesh=mesh, in_specs=in_specs, out_specs=(rows, rows, rows), check_vma=False
    )
```

```python
import functools

import jax
import jax.numpy as jnp
import ml_dtypes
import numpy as np
from jax import lax
from jax.experimental import pallas as pl
from jax.experimental.pallas import tpu as pltpu
from jax.sharding import PartitionSpec as P

NP = 8
PTS = NP**3
SQ = NP * NP
SMOOTH = 0.125
MESH = pl.DeviceIdType.MESH
F32 = jnp.float32
BF16 = jnp.bfloat16


def derivative_table(points):
    nodes = -np.cos(np.pi * np.arange(points) / (points - 1))
    end_weights = np.ones(points)
    end_weights[0] = 2.0
    end_weights[-1] = 2.0
    table = np.zeros((points, points))
    for i in range(points):
        for j in range(points):
            if i != j:
                table[i, j] = (
                    end_weights[i] / end_weights[j] * (-1.0) ** (i + j) / (nodes[i] - nodes[j])
                )
        table[i, i] = -np.sum(table[i])
    return nodes, table


def halves(x):
    x = np.asarray(x, np.float32)
    hi = x.astype(ml_dtypes.bfloat16)
    lo = (x - hi.astype(np.float32)).astype(ml_dtypes.bfloat16)
    return hi, lo


def tables(nh):
    nodes, deriv = derivative_table(NP)
    unit = np.eye(NP)
    k0 = np.kron(deriv, np.eye(SQ))
    k1 = np.kron(np.eye(4), np.kron(deriv, unit))
    k2 = np.kron(np.eye(4 * NP), deriv)
    hats = np.stack([(1.0 - nodes) / 2.0, (1.0 + nodes) / 2.0]).T
    raw = (
        hats[:, None, None, :, None, None]
        * hats[None, :, None, None, :, None]
        * hats[None, None, :, None, None, :]
    ).reshape(PTS, 8)
    corner = raw / raw.sum(axis=0, keepdims=True)
    grid = np.arange(PTS).reshape(NP, NP, NP)
    inner = [grid[:, 0], grid[:, -1], grid[:, :, 0], grid[:, :, -1]]
    sel = np.zeros((PTS, 4 * SQ), np.float32)
    spread = np.zeros((4 * 2 * SQ, PTS), np.float32)
    for s, side in enumerate(inner):
        for j, p in enumerate(side.ravel()):
            sel[p, s * SQ + j] = 1.0
            spread[s * 2 * SQ + j, p] = 1.0
            spread[s * 2 * SQ + SQ + j, p] = 1.0
    k0h, k0l = halves(k0)
    k1h, k1l = halves(k1)
    k2h, k2l = halves(k2)
    wh, wl = halves(np.repeat(corner, nh, axis=1))
    w = np.concatenate([wh, wl], axis=1)
    hh, hl = halves(np.repeat(raw.T, nh, axis=0))
    hh = np.concatenate([hh, hh], axis=0)
    hl = np.concatenate([hl, hl], axis=0)
    one = ml_dtypes.bfloat16
    return (
        np.stack([k0h, k0l]),
        np.stack([k1h, k1l]),
        np.stack([k2h, k2l]),
        sel.astype(one),
        spread.astype(one),
        w,
        np.stack([hh, hl]),
    )


NN = (((1,), (0,)), ((), ()))
NT = (((1,), (1,)), ((), ()))
TN = (((0,), (0,)), ((), ()))


def mm(a, b, dims=NN):
    return lax.dot_general(a, b, dims, preferred_element_type=F32)


def split(x):
    hi = x.astype(BF16)
    lo = (x - hi.astype(F32)).astype(BF16)
    return hi, lo


def iota(shape, dim):
    return lax.broadcasted_iota(jnp.int32, shape, dim)


def kernel(
    n_elem, n_sub, sections, width, nh,
    rhs_ref, scale_ref, helm_hbm, geo_hbm, inv_hbm, vid_ref, partner_ref, slots_ref,
    k0_hbm, k1_hbm, k2_hbm, sel_ref, spread_ref, w_ref, hat_ref,
    x_ref, r_ref, d_ref,
    gather, scatter, stacked, arrived, degree, corner_low, corner_high, inv_half,
    fsend, frecv, part, solved_slots, total_slots,
    fsend_sem, frecv_sem, psend_sem, precv_sem, ssend_sem, srecv_sem, tsend_sem, trecv_sem,
    inv_ref, helm_ref, geo_ref, k0_ref, k1_ref, k2_ref, load_sem,
):
    loads = [
        pltpu.make_async_copy(src, dst, load_sem.at[k])
        for k, (src, dst) in enumerate(
            (
                (inv_hbm, inv_ref), (k0_hbm, k0_ref), (geo_hbm, geo_ref),
                (helm_hbm, helm_ref), (k1_hbm, k1_ref), (k2_hbm, k2_ref),
            )
        )
    ]
    for load in loads:
        load.start()
    count = rhs_ref.shape[0]
    half = width // 2
    devices = n_elem * n_sub
    ch = 8 * nh
    elem = lax.axis_index("elem")
    sub = lax.axis_index("sub")
    me = elem * n_sub + sub

    def other(j):
        p = lax.rem(me + j, devices)
        return {"elem": lax.div(p, n_sub), "sub": lax.rem(p, n_sub)}

    barrier = pltpu.get_barrier_semaphore()

    def greet(j, carry):
        pl.semaphore_signal(barrier, inc=1, device_id=other(j), device_id_type=MESH)
        return carry

    lax.fori_loop(1, devices, greet, 0)

    low = iota((1, 128), 1) < SQ

    for b in range(sections):
        hit = partner_ref[b : b + 1, :] == iota((width, width), 0)
        order = jnp.sum(
            jnp.where(hit, slots_ref[b : b + 1, :].astype(F32), 0.0), axis=1, keepdims=True
        ).astype(jnp.int32)
        gather[b * width : (b + 1) * width, :] = jnp.where(
            order == iota((width, 6 * count), 1), 1.0, 0.0
        ).astype(BF16)
    slot_row = jnp.concatenate([slots_ref[b : b + 1, :] for b in range(sections)], axis=1)
    for s in range(6):
        scatter[s * count : (s + 1) * count, :] = jnp.where(
            slot_row - s * count == iota((count, sections * width), 0), 1.0, 0.0
        ).astype(BF16)

    vid = vid_ref[...]
    vid_high = lax.div(vid, 128)
    vid_low = vid - 128 * vid_high
    wide = iota((8, 8 * 128), 1)
    expand_low = jnp.where(lax.div(wide, 128) == iota((8, 8 * 128), 0), 1.0, 0.0)
    spread_low = mm(vid_low.astype(F32), expand_low, TN).astype(jnp.int32)
    corner_low[...] = jnp.where(
        spread_low == lax.rem(iota((count, 8 * 128), 1), 128), 1.0, 0.0
    ).astype(BF16)
    pair = iota((8, 2 * ch), 1)
    expand_high = jnp.where(lax.div(lax.rem(pair, ch), nh) == iota((8, 2 * ch), 0), 1.0, 0.0)
    spread_high = mm(vid_high.astype(F32), expand_high, TN).astype(jnp.int32)
    corner_high[...] = jnp.where(spread_high == lax.rem(iota((count, 2 * ch), 1), nh), 1.0, 0.0)

    def scatter_faces():
        flat = mm(scatter[...], arrived[...])
        sides = [flat[s * count : (s + 1) * count, :] for s in range(6)]
        inner = jnp.concatenate(sides[2:], axis=1).astype(BF16)
        result = mm(inner, spread_ref[...])
        first = sides[0] + pltpu.roll(sides[0], SQ, 1)
        last = sides[1] + pltpu.roll(sides[1], SQ, 1)
        return jnp.concatenate(
            [
                result[:, :128] + jnp.where(low, first, 0.0),
                result[:, 128 : PTS - 128],
                result[:, PTS - 128 :] + jnp.where(low, 0.0, last),
            ],
            axis=1,
        )

    arrived[...] = jnp.broadcast_to(jnp.where(low, 1.0, 0.0), arrived.shape).astype(BF16)
    degree[...] = scatter_faces()

    for load in loads:
        load.wait()
    inv_h, inv_l = split(inv_ref[...])
    inv_half[0] = inv_h
    inv_half[1] = inv_l

    pl.semaphore_wait(barrier, devices - 1)

    pending = []
    inner_bits = n_sub.bit_length() - 1
    send_order = list(reversed(range(inner_bits))) + list(range(inner_bits, sections))

    def send_faces(step, v):
        hi = v.astype(BF16)
        hi_f = hi.astype(F32)
        lo_f = v - hi_f
        picked = mm(jnp.concatenate([hi, lo_f.astype(BF16)], axis=0), sel_ref[...])

        def lower(h, l):
            return jnp.where(low, h, pltpu.roll(l, SQ, 1)).astype(BF16)

        def upper(h, l):
            return jnp.where(low, pltpu.roll(h, SQ, 1), l).astype(BF16)

        stacked[0:count, :] = lower(hi_f[:, :128], lo_f[:, :128])
        stacked[count : 2 * count, :] = upper(hi_f[:, PTS - 128 :], lo_f[:, PTS - 128 :])
        for s in range(2):
            h = picked[:count, 128 * s : 128 * s + 128]
            l = picked[count:, 128 * s : 128 * s + 128]
            stacked[(2 + 2 * s) * count : (3 + 2 * s) * count, :] = lower(h, l)
            stacked[(3 + 2 * s) * count : (4 + 2 * s) * count, :] = upper(h, l)
        for b in send_order:
            rows = mm(gather[b * width : (b + 1) * width, :], stacked[...])
            rows = rows + pltpu.roll(rows, SQ, 1)
            fsend[step, b] = jnp.where(low, rows[:half], rows[half:])
            bit = lax.rem(lax.div(me, 2**b), 2)
            p = me + (1 - 2 * bit) * 2**b
            copy = pltpu.make_async_remote_copy(
                src_ref=fsend.at[step, b],
                dst_ref=frecv.at[step, b],
                send_sem=fsend_sem.at[step, b],
                recv_sem=frecv_sem.at[step, b],
                device_id={"elem": lax.div(p, n_sub), "sub": lax.rem(p, n_sub)},
                device_id_type=MESH,
            )
            copy.start()
            pending.append(copy)

    def neighbours(step):
        for b in reversed(send_order):
            pltpu.make_async_copy(
                frecv.at[step, b], frecv.at[step, b], frecv_sem.at[step, b]
            ).wait()
            v = frecv[step, b]
            hi = v.astype(BF16).astype(F32)
            lo = v - hi
            arrived[b * width : b * width + half, :] = jnp.where(
                low, hi, pltpu.roll(lo, SQ, 1)
            ).astype(BF16)
            arrived[b * width + half : (b + 1) * width, :] = jnp.where(
                low, pltpu.roll(hi, SQ, 1), lo
            ).astype(BF16)
        return scatter_faces()

    def to_sub_peers(step, slots, index_of, send_sem, recv_sem):
        for j in range(1, n_sub):
            copy = pltpu.make_async_remote_copy(
                src_ref=slots.at[step, index_of(0)],
                dst_ref=slots.at[step, index_of(j)],
                send_sem=send_sem.at[step, j],
                recv_sem=recv_sem.at[step, j],
                device_id={"elem": elem, "sub": lax.rem(sub + j, n_sub)},
                device_id_type=MESH,
            )
            copy.start()
            pending.append(copy)

    def wait_sub_peers(step, slots, recv_sem):
        for j in range(1, n_sub):
            pltpu.make_async_copy(slots.at[step, 0], slots.at[step, 0], recv_sem.at[step, j]).wait()

    def send_corners(step, r):
        hi, lo = split(r)
        y = mm(hi, w_ref[...]) + mm(lo, w_ref[...])
        y = (y + pltpu.roll(y, ch, 1)) * corner_high[...]
        hi = y.astype(BF16).astype(F32)
        both = jnp.where(iota((1, 2 * ch), 1) < ch, hi, y - hi).astype(BF16)
        products = mm(both, corner_low[...], TN)
        total = None
        for k in range(2):
            for c in range(8):
                piece = products[k * ch + c * nh : k * ch + (c + 1) * nh, 128 * c : 128 * c + 128]
                total = piece if total is None else total + piece
        part[step, 0] = total
        to_sub_peers(step, part, lambda j: j, psend_sem, precv_sem)

    def solve(step):
        wait_sub_peers(step, part, precv_sem)
        total = part[step, 0]
        for j in range(1, n_sub):
            total = total + part[step, j]
        hi = total.astype(BF16).astype(F32)
        lo = total - hi
        row_h = jnp.concatenate([hi[h : h + 1, :] for h in range(nh)], axis=1)
        row_l = jnp.concatenate([lo[h : h + 1, :] for h in range(nh)], axis=1)
        rows = jnp.concatenate([row_h, row_l, jnp.zeros((14, nh * 128), F32)], axis=0).astype(BF16)
        out = mm(rows, inv_half[0], NT) + mm(rows, inv_half[1], NT)
        out = out[0:1] + out[1:2]
        own = [out[:, 128 * k : 128 * k + 128] for k in range(out.shape[1] // 128)]
        own.append(jnp.zeros((8 - len(own), 128), F32))
        solved_slots[step, sub] = jnp.concatenate(own, axis=0)
        to_sub_peers(step, solved_slots, lambda j: sub, ssend_sem, srecv_sem)

    def coarse(step):
        wait_sub_peers(step, solved_slots, srecv_sem)
        each = nh // n_sub
        solved = jnp.concatenate([solved_slots[step, j, 0:each, :] for j in range(n_sub)], axis=0)
        hi = solved.astype(BF16).astype(F32)
        lo = solved - hi
        keep = lax.div(iota((ch, 8 * 128), 0), nh) == lax.div(iota((ch, 8 * 128), 1), 128)

        def blocks(x):
            column = jnp.concatenate([x] * 8, axis=0)
            return jnp.where(keep, jnp.concatenate([column] * 8, axis=1), 0.0).astype(BF16)

        spread = jnp.concatenate([blocks(hi), blocks(lo)], axis=0)
        picked = (mm(corner_low[...], spread, NT) * corner_high[...]).astype(BF16)
        return mm(picked, hat_ref[0]) + mm(picked, hat_ref[1])

    def local(v):
        n2 = PTS // 2
        hi, lo = split(v)
        k0h, k0l = k0_ref[0], k0_ref[1]

        def two(x):
            return jnp.concatenate([x[:, :n2], x[:, n2:]], axis=0)

        def three(h, l, kh, kl, dims):
            return mm(h, kh, dims) + mm(l, kh, dims) + mm(h, kl, dims)

        slope = geo_ref[0] * three(hi, lo, k0h, k0l, NT)
        sh, sl = split(slope)
        total = helm_ref[...] * v + three(sh, sl, k0h, k0l, NN)
        hi2, lo2 = two(hi), two(lo)
        rest = None
        for d, k in ((1, k1_ref), (2, k2_ref)):
            slope = two(geo_ref[d]) * three(hi2, lo2, k[0], k[1], NT)
            sh, sl = split(slope)
            piece = three(sh, sl, k[0], k[1], NN)
            rest = piece if rest is None else rest + piece
        return total + jnp.concatenate([rest[:count], rest[count:]], axis=1)

    def inner(a, b):
        return jnp.sum(a * b, axis=0, keepdims=True)

    def narrow(x):
        total = x[:, :128]
        for k in range(1, PTS // 128):
            total = total + x[:, 128 * k : 128 * k + 128]
        return total

    def send_totals(step, pairs):
        rows = [narrow(inner(a, b)) for a, b in pairs]
        rows.append(jnp.zeros((8 - len(rows), 128), F32))
        total_slots[step, 0] = jnp.concatenate(rows, axis=0)

        def start(j, carry):
            pltpu.make_async_remote_copy(
                src_ref=total_slots.at[step, 0],
                dst_ref=total_slots.at[step, j],
                send_sem=tsend_sem.at[step],
                recv_sem=trecv_sem.at[step],
                device_id=other(j),
                device_id_type=MESH,
            ).start()
            return carry

        lax.fori_loop(1, devices, start, 0)

    def totals(step, many):
        others = total_slots.at[step, pl.ds(1, devices - 1)]
        pltpu.make_async_copy(others, others, trecv_sem.at[step]).wait()
        whole = jnp.sum(total_slots[step], axis=0)
        sums = jnp.sum(whole, axis=1, keepdims=True)
        return [sums[k : k + 1] for k in range(many)]

    scale = scale_ref[...]

    def smooth_of(y, step):
        return scale * (y - SMOOTH * (degree[...] * y - neighbours(step)))

    def precondition(v, faces, step):
        y = scale * v
        send_corners(step, v)
        send_faces(faces, y)
        solve(step)
        smooth = smooth_of(y, faces)
        return smooth + coarse(step)

    def operator(v, step):
        send_faces(step, v)
        inside = local(v) + degree[...] * v
        return inside - neighbours(step)

    r0 = rhs_ref[...]
    z0 = precondition(r0, 0, 0)
    w0 = operator(z0, 1)
    send_totals(0, [(r0, z0), (z0, w0)])
    q0 = precondition(w0, 2, 1)
    rz0, dw0 = totals(0, 2)
    alpha0 = rz0 / dw0
    r1 = r0 - alpha0 * w0
    z1 = z0 - alpha0 * q0
    u1 = operator(z1, 3)
    send_totals(1, [(r1, z1), (z1, u1), (z1, w0), (z0, u1)])
    q1 = precondition(u1, 4, 2)
    rz1, zu, zw, du = totals(1, 4)
    beta0 = rz1 / rz0
    dw1 = zu + beta0 * (zw + du) + beta0 * beta0 * dw0
    alpha1 = rz1 / dw1
    d1 = z1 + beta0 * z0
    r2 = r1 - alpha1 * (u1 + beta0 * w0)
    z2 = z1 - alpha1 * (q1 + beta0 * q0)
    send_totals(2, [(r2, z2)])
    x_ref[...] = alpha0 * z0 + alpha1 * d1
    r_ref[...] = r2
    (rz2,) = totals(2, 1)
    d_ref[...] = z2 + (rz2 / rz1) * d1

    for copy in pending:
        copy.wait_send()
    for step in range(3):
        others = total_slots.at[step, pl.ds(1, devices - 1)]
        pltpu.make_async_copy(others, others, tsend_sem.at[step]).wait()


def hand_over(x_ref, r_ref, d_ref, x_out, r_out, d_out, sem):
    rows = x_ref.shape[0] // 4
    copies = []
    for k, (src, dst) in enumerate(((x_ref, x_out), (r_ref, r_out), (d_ref, d_out))):
        for q in range(4):
            block = pl.ds(q * rows, rows)
            copies.append(pltpu.make_async_copy(src.at[block], dst.at[block], sem.at[k, q]))
    for copy in copies:
        copy.start()
    for copy in copies:
        copy.wait()


def on_device(
    n_elem, n_sub,
    right_side, smoother_scale, helmholtz, geometry, coarse_inverse, vertex_ids, face_slot, face_partner,
):
    count = right_side.shape[0]
    _, sections, width = face_slot.shape
    half = width // 2
    nv = coarse_inverse.shape[2]
    nh = nv // 128
    devices = n_elem * n_sub
    constants = [jnp.asarray(t) for t in tables(nh)]
    vmem = pl.BlockSpec(memory_space=pltpu.VMEM)
    hbm = pl.BlockSpec(memory_space=pl.ANY)
    field = jax.ShapeDtypeStruct((count, PTS), F32)
    dma = pltpu.SemaphoreType.DMA
    operands = (
        right_side, smoother_scale, helmholtz, geometry, coarse_inverse[0], vertex_ids,
        face_partner[0], face_slot[0], *constants,
    )
    results = pl.pallas_call(
        functools.partial(kernel, n_elem, n_sub, sections, width, nh),
        out_shape=(field, field, field),
        in_specs=[hbm if k in (2, 3, 4, 8, 9, 10) else vmem for k in range(len(operands))],
        out_specs=(vmem, vmem, vmem),
        scratch_shapes=[
            pltpu.VMEM((sections * width, 6 * count), BF16),
            pltpu.VMEM((6 * count, sections * width), BF16),
            pltpu.VMEM((6 * count, 128), BF16),
            pltpu.VMEM((sections * width, 128), BF16),
            pltpu.VMEM((count, PTS), F32),
            pltpu.VMEM((count, 8 * 128), BF16),
            pltpu.VMEM((count, 16 * nh), F32),
            pltpu.VMEM((2,) + coarse_inverse.shape[1:], BF16),
            pltpu.VMEM((5, sections, half, 128), F32),
            pltpu.VMEM((5, sections, half, 128), F32),
            pltpu.VMEM((3, n_sub, nh, 128), F32),
            pltpu.VMEM((3, n_sub, 8, 128), F32),
            pltpu.VMEM((3, devices, 8, 128), F32),
            dma((5, sections)),
            dma((5, sections)),
            dma((3, n_sub)),
            dma((3, n_sub)),
            dma((3, n_sub)),
            dma((3, n_sub)),
            dma((3,)),
            dma((3,)),
            pltpu.VMEM(coarse_inverse.shape[1:], F32),
            pltpu.VMEM((count, PTS), F32),
            pltpu.VMEM((3, count, PTS), F32),
            pltpu.VMEM((2, PTS, PTS), BF16),
            pltpu.VMEM((2, PTS // 2, PTS // 2), BF16),
            pltpu.VMEM((2, PTS // 2, PTS // 2), BF16),
            dma((6,)),
        ],
        compiler_params=pltpu.CompilerParams(
            collective_id=0, has_side_effects=True, vmem_limit_bytes=56 * 2**20
        ),
        cost_estimate=pl.CostEstimate(flops=2 * 10**10, bytes_accessed=8 * 10**6, transcendentals=0),
    )(*operands)
    return pl.pallas_call(
        hand_over,
        out_shape=(field, field, field),
        in_specs=[hbm] * 3,
        out_specs=(hbm, hbm, hbm),
        scratch_shapes=[dma((3, 4))],
        compiler_params=pltpu.CompilerParams(vmem_limit_bytes=56 * 2**20),
        cost_estimate=pl.CostEstimate(flops=0, bytes_accessed=3 * 2**20, transcendentals=0),
    )(*results)


def solution(mesh):
    rows = P(("variant", "elem", "sub"), None)
    in_specs = (
        rows,
        rows,
        rows,
        P(None, ("variant", "elem", "sub"), None),
        P(("variant", "elem"), "sub", None),
        P(None, ("elem", "sub")),
        P(("elem", "sub"), None, None),
        P(("elem", "sub"), None, None),
    )
    body = functools.partial(on_device, mesh.shape["elem"], mesh.shape["sub"])
    return jax.shard_map(
        body, mesh=mesh, in_specs=in_specs, out_specs=(rows, rows, rows), check_vma=False
    )
```

```python
import functools

import jax
import jax.numpy as jnp
import ml_dtypes
import numpy as np
from jax import lax
from jax.experimental import pallas as pl
from jax.experimental.pallas import tpu as pltpu
from jax.sharding import PartitionSpec as P

NP = 8
PTS = NP**3
SQ = NP * NP
SMOOTH = 0.125
MESH = pl.DeviceIdType.MESH
F32 = jnp.float32
BF16 = jnp.bfloat16


def derivative_table(points):
    nodes = -np.cos(np.pi * np.arange(points) / (points - 1))
    end_weights = np.ones(points)
    end_weights[0] = 2.0
    end_weights[-1] = 2.0
    table = np.zeros((points, points))
    for i in range(points):
        for j in range(points):
            if i != j:
                table[i, j] = (
                    end_weights[i] / end_weights[j] * (-1.0) ** (i + j) / (nodes[i] - nodes[j])
                )
        table[i, i] = -np.sum(table[i])
    return nodes, table


def halves(x):
    x = np.asarray(x, np.float32)
    hi = x.astype(ml_dtypes.bfloat16)
    lo = (x - hi.astype(np.float32)).astype(ml_dtypes.bfloat16)
    return hi, lo


def tables(nh):
    nodes, deriv = derivative_table(NP)
    unit = np.eye(NP)
    k0 = np.kron(deriv, np.eye(SQ))
    k1 = np.kron(np.eye(4), np.kron(deriv, unit))
    k2 = np.kron(np.eye(4 * NP), deriv)
    hats = np.stack([(1.0 - nodes) / 2.0, (1.0 + nodes) / 2.0]).T
    raw = (
        hats[:, None, None, :, None, None]
        * hats[None, :, None, None, :, None]
        * hats[None, None, :, None, None, :]
    ).reshape(PTS, 8)
    corner = raw / raw.sum(axis=0, keepdims=True)
    grid = np.arange(PTS).reshape(NP, NP, NP)
    inner = [grid[:, 0], grid[:, -1], grid[:, :, 0], grid[:, :, -1]]
    sel = np.zeros((PTS, 4 * SQ), np.float32)
    spread = np.zeros((4 * 2 * SQ, PTS), np.float32)
    for s, side in enumerate(inner):
        for j, p in enumerate(side.ravel()):
            sel[p, s * SQ + j] = 1.0
            spread[s * 2 * SQ + j, p] = 1.0
            spread[s * 2 * SQ + SQ + j, p] = 1.0
    k0h, k0l = halves(k0)
    k1h, k1l = halves(k1)
    k2h, k2l = halves(k2)
    wh, wl = halves(np.repeat(corner, nh, axis=1))
    w = np.concatenate([wh, wl], axis=1)
    hh, hl = halves(np.repeat(raw.T, nh, axis=0))
    hh = np.concatenate([hh, hh], axis=0)
    hl = np.concatenate([hl, hl], axis=0)
    one = ml_dtypes.bfloat16
    return (
        np.stack([k0h, k0l]),
        np.stack([k1h, k1l]),
        np.stack([k2h, k2l]),
        sel.astype(one),
        spread.astype(one),
        w,
        np.stack([hh, hl]),
    )


NN = (((1,), (0,)), ((), ()))
NT = (((1,), (1,)), ((), ()))
TN = (((0,), (0,)), ((), ()))


def mm(a, b, dims=NN):
    return lax.dot_general(a, b, dims, preferred_element_type=F32)


def split(x):
    hi = x.astype(BF16)
    lo = (x - hi.astype(F32)).astype(BF16)
    return hi, lo


def iota(shape, dim):
    return lax.broadcasted_iota(jnp.int32, shape, dim)


def kernel(
    n_elem, n_sub, sections, width, nh,
    rhs_ref, scale_ref, helm_hbm, geo_hbm, inv_hbm, vid_ref, partner_ref, slots_ref,
    k0_hbm, k1_hbm, k2_hbm, sel_ref, spread_ref, w_ref, hat_ref,
    x_ref, r_ref, d_ref,
    gather, scatter, stacked, arrived, degree, corner_low, corner_high, inv_half,
    fsend, frecv, part, solved_slots, total_slots,
    fsend_sem, frecv_sem, psend_sem, precv_sem, ssend_sem, srecv_sem, tsend_sem, trecv_sem,
    inv_ref, helm_ref, geo_ref, k0_ref, k1_ref, k2_ref, load_sem,
):
    loads = [
        pltpu.make_async_copy(src, dst, load_sem.at[k])
        for k, (src, dst) in enumerate(
            (
                (inv_hbm, inv_ref), (k0_hbm, k0_ref), (geo_hbm, geo_ref),
                (helm_hbm, helm_ref), (k1_hbm, k1_ref), (k2_hbm, k2_ref),
            )
        )
    ]
    for load in loads:
        load.start()
    count = rhs_ref.shape[0]
    half = width // 2
    devices = n_elem * n_sub
    ch = 8 * nh
    elem = lax.axis_index("elem")
    sub = lax.axis_index("sub")
    me = elem * n_sub + sub

    def other(j):
        p = lax.rem(me + j, devices)
        return {"elem": lax.div(p, n_sub), "sub": lax.rem(p, n_sub)}

    barrier = pltpu.get_barrier_semaphore()

    def greet(j, carry):
        pl.semaphore_signal(barrier, inc=1, device_id=other(j), device_id_type=MESH)
        return carry

    lax.fori_loop(1, devices, greet, 0)

    low = iota((1, 128), 1) < SQ

    for b in range(sections):
        hit = partner_ref[b : b + 1, :] == iota((width, width), 0)
        order = jnp.sum(
            jnp.where(hit, slots_ref[b : b + 1, :].astype(F32), 0.0), axis=1, keepdims=True
        ).astype(jnp.int32)
        gather[b * width : (b + 1) * width, :] = jnp.where(
            order == iota((width, 6 * count), 1), 1.0, 0.0
        ).astype(BF16)
    slot_row = jnp.concatenate([slots_ref[b : b + 1, :] for b in range(sections)], axis=1)
    for s in range(6):
        scatter[s * count : (s + 1) * count, :] = jnp.where(
            slot_row - s * count == iota((count, sections * width), 0), 1.0, 0.0
        ).astype(BF16)

    vid = vid_ref[...]
    vid_high = lax.div(vid, 128)
    vid_low = vid - 128 * vid_high
    wide = iota((8, 8 * 128), 1)
    expand_low = jnp.where(lax.div(wide, 128) == iota((8, 8 * 128), 0), 1.0, 0.0)
    spread_low = mm(vid_low.astype(F32), expand_low, TN).astype(jnp.int32)
    corner_low[...] = jnp.where(
        spread_low == lax.rem(iota((count, 8 * 128), 1), 128), 1.0, 0.0
    ).astype(BF16)
    pair = iota((8, 2 * ch), 1)
    expand_high = jnp.where(lax.div(lax.rem(pair, ch), nh) == iota((8, 2 * ch), 0), 1.0, 0.0)
    spread_high = mm(vid_high.astype(F32), expand_high, TN).astype(jnp.int32)
    corner_high[...] = jnp.where(spread_high == lax.rem(iota((count, 2 * ch), 1), nh), 1.0, 0.0)

    def scatter_faces():
        flat = mm(scatter[...], arrived[...])
        sides = [flat[s * count : (s + 1) * count, :] for s in range(6)]
        inner = jnp.concatenate(sides[2:], axis=1).astype(BF16)
        result = mm(inner, spread_ref[...])
        first = sides[0] + pltpu.roll(sides[0], SQ, 1)
        last = sides[1] + pltpu.roll(sides[1], SQ, 1)
        return jnp.concatenate(
            [
                result[:, :128] + jnp.where(low, first, 0.0),
                result[:, 128 : PTS - 128],
                result[:, PTS - 128 :] + jnp.where(low, 0.0, last),
            ],
            axis=1,
        )

    arrived[...] = jnp.broadcast_to(jnp.where(low, 1.0, 0.0), arrived.shape).astype(BF16)
    degree[...] = scatter_faces()

    for load in loads:
        load.wait()
    inv_h, inv_l = split(inv_ref[...])
    inv_half[0] = inv_h
    inv_half[1] = inv_l

    pl.semaphore_wait(barrier, devices - 1)

    pending = []
    inner_bits = n_sub.bit_length() - 1
    send_order = list(reversed(range(inner_bits))) + list(range(inner_bits, sections))

    def send_faces(step, v):
        hi = v.astype(BF16)
        hi_f = hi.astype(F32)
        lo_f = v - hi_f
        picked = mm(jnp.concatenate([hi, lo_f.astype(BF16)], axis=0), sel_ref[...])

        def lower(h, l):
            return jnp.where(low, h, pltpu.roll(l, SQ, 1)).astype(BF16)

        def upper(h, l):
            return jnp.where(low, pltpu.roll(h, SQ, 1), l).astype(BF16)

        stacked[0:count, :] = lower(hi_f[:, :128], lo_f[:, :128])
        stacked[count : 2 * count, :] = upper(hi_f[:, PTS - 128 :], lo_f[:, PTS - 128 :])
        for s in range(2):
            h = picked[:count, 128 * s : 128 * s + 128]
            l = picked[count:, 128 * s : 128 * s + 128]
            stacked[(2 + 2 * s) * count : (3 + 2 * s) * count, :] = lower(h, l)
            stacked[(3 + 2 * s) * count : (4 + 2 * s) * count, :] = upper(h, l)
        for b in send_order:
            rows = mm(gather[b * width : (b + 1) * width, :], stacked[...])
            rows = rows + pltpu.roll(rows, SQ, 1)
            fsend[step, b] = jnp.where(low, rows[:half], rows[half:])
            bit = lax.rem(lax.div(me, 2**b), 2)
            p = me + (1 - 2 * bit) * 2**b
            copy = pltpu.make_async_remote_copy(
                src_ref=fsend.at[step, b],
                dst_ref=frecv.at[step, b],
                send_sem=fsend_sem.at[step, b],
                recv_sem=frecv_sem.at[step, b],
                device_id={"elem": lax.div(p, n_sub), "sub": lax.rem(p, n_sub)},
                device_id_type=MESH,
            )
            copy.start()
            pending.append(copy)

    def neighbours(step):
        for b in reversed(send_order):
            pltpu.make_async_copy(
                frecv.at[step, b], frecv.at[step, b], frecv_sem.at[step, b]
            ).wait()
            v = frecv[step, b]
            hi = v.astype(BF16).astype(F32)
            lo = v - hi
            arrived[b * width : b * width + half, :] = jnp.where(
                low, hi, pltpu.roll(lo, SQ, 1)
            ).astype(BF16)
            arrived[b * width + half : (b + 1) * width, :] = jnp.where(
                low, pltpu.roll(hi, SQ, 1), lo
            ).astype(BF16)
        return scatter_faces()

    def to_sub_peers(step, slots, index_of, send_sem, recv_sem):
        for j in range(1, n_sub):
            copy = pltpu.make_async_remote_copy(
                src_ref=slots.at[step, index_of(0)],
                dst_ref=slots.at[step, index_of(j)],
                send_sem=send_sem.at[step, j],
                recv_sem=recv_sem.at[step, j],
                device_id={"elem": elem, "sub": lax.rem(sub + j, n_sub)},
                device_id_type=MESH,
            )
            copy.start()
            pending.append(copy)

    def wait_sub_peers(step, slots, recv_sem):
        for j in range(1, n_sub):
            pltpu.make_async_copy(slots.at[step, 0], slots.at[step, 0], recv_sem.at[step, j]).wait()

    def send_corners(step, r):
        hi, lo = split(r)
        y = mm(hi, w_ref[...]) + mm(lo, w_ref[...])
        y = (y + pltpu.roll(y, ch, 1)) * corner_high[...]
        hi = y.astype(BF16).astype(F32)
        both = jnp.where(iota((1, 2 * ch), 1) < ch, hi, y - hi).astype(BF16)
        products = mm(both, corner_low[...], TN)
        total = None
        for k in range(2):
            for c in range(8):
                piece = products[k * ch + c * nh : k * ch + (c + 1) * nh, 128 * c : 128 * c + 128]
                total = piece if total is None else total + piece
        part[step, 0] = total
        to_sub_peers(step, part, lambda j: j, psend_sem, precv_sem)

    def solve(step):
        wait_sub_peers(step, part, precv_sem)
        total = part[step, 0]
        for j in range(1, n_sub):
            total = total + part[step, j]
        hi = total.astype(BF16).astype(F32)
        lo = total - hi
        row_h = jnp.concatenate([hi[h : h + 1, :] for h in range(nh)], axis=1)
        row_l = jnp.concatenate([lo[h : h + 1, :] for h in range(nh)], axis=1)
        rows = jnp.concatenate([row_h, row_l, jnp.zeros((14, nh * 128), F32)], axis=0).astype(BF16)
        out = mm(rows, inv_half[0], NT) + mm(rows, inv_half[1], NT)
        out = out[0:1] + out[1:2]
        own = [out[:, 128 * k : 128 * k + 128] for k in range(out.shape[1] // 128)]
        own.append(jnp.zeros((8 - len(own), 128), F32))
        solved_slots[step, sub] = jnp.concatenate(own, axis=0)
        to_sub_peers(step, solved_slots, lambda j: sub, ssend_sem, srecv_sem)

    def coarse(step):
        wait_sub_peers(step, solved_slots, srecv_sem)
        each = nh // n_sub
        solved = jnp.concatenate([solved_slots[step, j, 0:each, :] for j in range(n_sub)], axis=0)
        hi = solved.astype(BF16).astype(F32)
        lo = solved - hi
        keep = lax.div(iota((ch, 8 * 128), 0), nh) == lax.div(iota((ch, 8 * 128), 1), 128)

        def blocks(x):
            column = jnp.concatenate([x] * 8, axis=0)
            return jnp.where(keep, jnp.concatenate([column] * 8, axis=1), 0.0).astype(BF16)

        spread = jnp.concatenate([blocks(hi), blocks(lo)], axis=0)
        picked = (mm(corner_low[...], spread, NT) * corner_high[...]).astype(BF16)
        return mm(picked, hat_ref[0]) + mm(picked, hat_ref[1])

    def local(v):
        n2 = PTS // 2
        hi, lo = split(v)
        k0h, k0l = k0_ref[0], k0_ref[1]

        def two(x):
            return jnp.concatenate([x[:, :n2], x[:, n2:]], axis=0)

        def three(h, l, kh, kl, dims):
            return mm(h, kh, dims) + mm(l, kh, dims) + mm(h, kl, dims)

        slope = geo_ref[0] * three(hi, lo, k0h, k0l, NT)
        sh, sl = split(slope)
        total = helm_ref[...] * v + three(sh, sl, k0h, k0l, NN)
        hi2, lo2 = two(hi), two(lo)
        rest = None
        for d, k in ((1, k1_ref), (2, k2_ref)):
            slope = two(geo_ref[d]) * three(hi2, lo2, k[0], k[1], NT)
            sh, sl = split(slope)
            piece = three(sh, sl, k[0], k[1], NN)
            rest = piece if rest is None else rest + piece
        return total + jnp.concatenate([rest[:count], rest[count:]], axis=1)

    def inner(a, b):
        return jnp.sum(a * b, axis=0, keepdims=True)

    def narrow(x):
        total = x[:, :128]
        for k in range(1, PTS // 128):
            total = total + x[:, 128 * k : 128 * k + 128]
        return total

    def send_totals(step, pairs):
        rows = [narrow(inner(a, b)) for a, b in pairs]
        rows.append(jnp.zeros((8 - len(rows), 128), F32))
        total_slots[step, 0] = jnp.concatenate(rows, axis=0)

        def start(j, carry):
            pltpu.make_async_remote_copy(
                src_ref=total_slots.at[step, 0],
                dst_ref=total_slots.at[step, j],
                send_sem=tsend_sem.at[step],
                recv_sem=trecv_sem.at[step],
                device_id=other(j),
                device_id_type=MESH,
            ).start()
            return carry

        lax.fori_loop(1, devices, start, 0)

    def totals(step, many):
        others = total_slots.at[step, pl.ds(1, devices - 1)]
        pltpu.make_async_copy(others, others, trecv_sem.at[step]).wait()
        whole = jnp.sum(total_slots[step], axis=0)
        sums = jnp.sum(whole, axis=1, keepdims=True)
        return [sums[k : k + 1] for k in range(many)]

    scale = scale_ref[...]

    def smooth_of(y, step):
        return scale * (y - SMOOTH * (degree[...] * y - neighbours(step)))

    def precondition(v, faces, step):
        y = scale * v
        send_corners(step, v)
        send_faces(faces, y)
        solve(step)
        smooth = smooth_of(y, faces)
        return smooth + coarse(step)

    def operator(v, step):
        send_faces(step, v)
        inside = local(v) + degree[...] * v
        return inside - neighbours(step)

    r0 = rhs_ref[...]
    z0 = precondition(r0, 0, 0)
    w0 = operator(z0, 1)
    send_totals(0, [(r0, z0), (z0, w0)])
    q0 = precondition(w0, 2, 1)
    rz0, dw0 = totals(0, 2)
    alpha0 = rz0 / dw0
    r1 = r0 - alpha0 * w0
    z1 = z0 - alpha0 * q0
    u1 = operator(z1, 3)
    send_totals(1, [(r1, z1), (z1, u1), (z1, w0), (z0, u1)])
    q1 = precondition(u1, 4, 2)
    rz1, zu, zw, du = totals(1, 4)
    beta0 = rz1 / rz0
    dw1 = zu + beta0 * (zw + du) + beta0 * beta0 * dw0
    alpha1 = rz1 / dw1
    d1 = z1 + beta0 * z0
    r2 = r1 - alpha1 * (u1 + beta0 * w0)
    z2 = z1 - alpha1 * (q1 + beta0 * q0)
    send_totals(2, [(r2, z2)])
    x_ref[...] = alpha0 * z0 + alpha1 * d1
    r_ref[...] = r2
    (rz2,) = totals(2, 1)
    d_ref[...] = z2 + (rz2 / rz1) * d1

    for copy in pending:
        copy.wait_send()
    for step in range(3):
        others = total_slots.at[step, pl.ds(1, devices - 1)]
        pltpu.make_async_copy(others, others, tsend_sem.at[step]).wait()


def hand_over(x_ref, r_ref, d_ref, x_out, r_out, d_out):
    x_out[...] = x_ref[...]
    r_out[...] = r_ref[...]
    d_out[...] = d_ref[...]


def on_device(
    n_elem, n_sub,
    right_side, smoother_scale, helmholtz, geometry, coarse_inverse, vertex_ids, face_slot, face_partner,
):
    count = right_side.shape[0]
    _, sections, width = face_slot.shape
    half = width // 2
    nv = coarse_inverse.shape[2]
    nh = nv // 128
    devices = n_elem * n_sub
    constants = [jnp.asarray(t) for t in tables(nh)]
    vmem = pl.BlockSpec(memory_space=pltpu.VMEM)
    hbm = pl.BlockSpec(memory_space=pl.ANY)
    block = pl.BlockSpec((count // 2, PTS), lambda i: (i, 0))
    field = jax.ShapeDtypeStruct((count, PTS), F32)
    dma = pltpu.SemaphoreType.DMA
    operands = (
        right_side, smoother_scale, helmholtz, geometry, coarse_inverse[0], vertex_ids,
        face_partner[0], face_slot[0], *constants,
    )
    results = pl.pallas_call(
        functools.partial(kernel, n_elem, n_sub, sections, width, nh),
        out_shape=(field, field, field),
        in_specs=[hbm if k in (2, 3, 4, 8, 9, 10) else vmem for k in range(len(operands))],
        out_specs=(vmem, vmem, vmem),
        scratch_shapes=[
            pltpu.VMEM((sections * width, 6 * count), BF16),
            pltpu.VMEM((6 * count, sections * width), BF16),
            pltpu.VMEM((6 * count, 128), BF16),
            pltpu.VMEM((sections * width, 128), BF16),
            pltpu.VMEM((count, PTS), F32),
            pltpu.VMEM((count, 8 * 128), BF16),
            pltpu.VMEM((count, 16 * nh), F32),
            pltpu.VMEM((2,) + coarse_inverse.shape[1:], BF16),
            pltpu.VMEM((5, sections, half, 128), F32),
            pltpu.VMEM((5, sections, half, 128), F32),
            pltpu.VMEM((3, n_sub, nh, 128), F32),
            pltpu.VMEM((3, n_sub, 8, 128), F32),
            pltpu.VMEM((3, devices, 8, 128), F32),
            dma((5, sections)),
            dma((5, sections)),
            dma((3, n_sub)),
            dma((3, n_sub)),
            dma((3, n_sub)),
            dma((3, n_sub)),
            dma((3,)),
            dma((3,)),
            pltpu.VMEM(coarse_inverse.shape[1:], F32),
            pltpu.VMEM((count, PTS), F32),
            pltpu.VMEM((3, count, PTS), F32),
            pltpu.VMEM((2, PTS, PTS), BF16),
            pltpu.VMEM((2, PTS // 2, PTS // 2), BF16),
            pltpu.VMEM((2, PTS // 2, PTS // 2), BF16),
            dma((6,)),
        ],
        compiler_params=pltpu.CompilerParams(
            collective_id=0, has_side_effects=True, vmem_limit_bytes=56 * 2**20
        ),
        cost_estimate=pl.CostEstimate(flops=2 * 10**10, bytes_accessed=8 * 10**6, transcendentals=0),
    )(*operands)
    return pl.pallas_call(
        hand_over,
        out_shape=(field, field, field),
        grid=(2,),
        in_specs=[block] * 3,
        out_specs=(block, block, block),
        compiler_params=pltpu.CompilerParams(vmem_limit_bytes=56 * 2**20),
        cost_estimate=pl.CostEstimate(flops=0, bytes_accessed=3 * 2**20, transcendentals=0),
    )(*results)


def solution(mesh):
    rows = P(("variant", "elem", "sub"), None)
    in_specs = (
        rows,
        rows,
        rows,
        P(None, ("variant", "elem", "sub"), None),
        P(("variant", "elem"), "sub", None),
        P(None, ("elem", "sub")),
        P(("elem", "sub"), None, None),
        P(("elem", "sub"), None, None),
    )
    body = functools.partial(on_device, mesh.shape["elem"], mesh.shape["sub"])
    return jax.shard_map(
        body, mesh=mesh, in_specs=in_specs, out_specs=(rows, rows, rows), check_vma=False
    )
```
